32 devices in a mesh: wide: 8 (over y, x, core), narrow: 4 (over z).
Axes of the slice: x: 2, y: 2, z: 4, core: 2. Of those that a mesh axis runs over, the one named last changes fastest.
Arguments:
- tokens: bfloat16 [16384, 768], P('wide'), may hold values from -6 to 6
- cotangent: bfloat16 [16384, 768], P('wide'), may hold values from -6 to 6
- lengths: int32 [8, 4], P('wide'), may hold values from 0 to 2048, as said below
- query_weight: bfloat16 [768, 768], P(None, 'narrow'), may hold values from -0.21875 to 0.21875
- query_bias: bfloat16 [768], P('narrow'), may hold values from -2 to 2
- key_weight: bfloat16 [768, 768], P(None, 'narrow'), may hold values from -0.21875 to 0.21875
- key_bias: bfloat16 [768], P('narrow'), may hold values from -2 to 2
- value_weight: bfloat16 [768, 768], P(None, 'narrow'), may hold values from -0.21875 to 0.21875
- value_bias: bfloat16 [768], P('narrow'), may hold values from -2 to 2
- out_weight: bfloat16 [768, 768], P('narrow'), may hold values from -0.875 to 0.875
- out_bias: bfloat16 [768], replicated, may hold values from -2 to 2
- norm_gain: bfloat16 [768], replicated, may hold values from 0.5 to 1.5
- norm_shift: bfloat16 [768], replicated, may hold values from -2 to 2
- up_weight: bfloat16 [768, 3072], P(None, 'narrow'), may hold values from -0.21875 to 0.21875
- up_bias: bfloat16 [3072], P('narrow'), may hold values from -2 to 2
- down_weight: bfloat16 [3072, 768], P('narrow'), may hold values from -0.109375 to 0.109375
- down_bias: bfloat16 [768], replicated, may hold values from -2 to 2
- final_gain: bfloat16 [768], replicated, may hold values from 0.5 to 1.5
- final_shift: bfloat16 [768], replicated, may hold values from -2 to 2
Outputs:
- layer_out: bfloat16 [16384, 768], P('wide')
- tokens_grad: float32 [16384, 768], P('wide')
- queryweight_grad: float32 [768, 768], P(None, 'narrow')
- querybias_grad: float32 [768], P('narrow')
- keyweight_grad: float32 [768, 768], P(None, 'narrow')
- keybias_grad: float32 [768], P('narrow')
- valueweight_grad: float32 [768, 768], P(None, 'narrow')
- valuebias_grad: float32 [768], P('narrow')
- outweight_grad: float32 [768, 768], P('narrow')
- outbias_grad: float32 [768], replicated
- normgain_grad: float32 [768], replicated
- normshift_grad: float32 [768], replicated
- upweight_grad: float32 [768, 3072], P(None, 'narrow')
- upbias_grad: float32 [3072], P('narrow')
- downweight_grad: float32 [3072, 768], P('narrow')
- downbias_grad: float32 [768], replicated
- finalgain_grad: float32 [768], replicated
- finalshift_grad: float32 [768], replicated
The draws below stay inside these ranges and needn't reach their ends.
Inputs may be any that keep to these rules, and one draw needn't show every extreme that they name: `lengths`: in each row the first few slots hold sequences of 64 tokens or more and the remaining slots are 0; a row sums to at most 2048; in every draw one row is a single sequence of 2048 tokens.
All inputs are finite; a program needn't handle non-finite values.
Results may differ from the reference program's by a relative error of at most 0.014.
Values sent between devices are 32-bit elements; how exact they have to be, the bound alone decides.
No kernel may reach another device: no remote copies, remote signals or barrier semaphores. Data moves between devices by JAX's collectives and lax.ppermute only.
A program may use at most 256 MiB of HBM per device.

```python
import math
import jax
import jax.numpy as jnp
from jax import lax

D = 768
HEADS = 12
HEAD = 64
FF = 3072
CAP = 2048
SLOTS = 4
MIN_LEN = 64
GROUPS = 8
TOKENS = 16384


def draw_lengths(key, part):
    key = jax.random.fold_in(key, 7)
    keys = jax.random.split(key, 4)
    spread_draw = jax.random.randint(keys[0], (GROUPS,), 0, 4096)
    skewed = spread_draw * spread_draw // 4096
    seq_count = jax.random.randint(keys[1], (GROUPS,), 1, SLOTS + 1)
    chosen = jax.random.randint(keys[2], (), 0, GROUPS)
    row_ids = jnp.arange(GROUPS)
    seq_count = jnp.where(row_ids == chosen, 1, seq_count)
    spare = CAP - seq_count * MIN_LEN
    extra = jnp.where(row_ids == chosen, spare, skewed * spare // 4096)
    slot_ids = jnp.arange(SLOTS)
    used = slot_ids[None, :] < seq_count[:, None]
    weights = jnp.where(used, jax.random.randint(keys[3], (GROUPS, SLOTS), 1, 1000), 0)
    shares = extra[:, None] * weights // jnp.sum(weights, axis=1, keepdims=True)
    leftover = extra - jnp.sum(shares, axis=1)
    shares = shares + jnp.where(slot_ids[None, :] == 0, leftover[:, None], 0)
    return jnp.where(used, MIN_LEN + shares, 0).astype(jnp.int32)


def block_scale(key, extent, cuts, smallest, largest):
    def one(dim, blocks):
        steps = jax.random.uniform(jax.random.fold_in(jax.random.fold_in(key, 6), dim), (blocks,), jnp.float32, smallest / len(cuts), largest / len(cuts))
        return jnp.repeat(jnp.exp(steps), extent[dim] // blocks).reshape((-1,) + (1,) * (len(extent) - dim - 1))

    loudness = one(*cuts[0])
    for cut in cuts[1:]:
        loudness = loudness * one(*cut)
    return loudness


def centred(key, extent, width, most, shards=(), kind=jnp.bfloat16):
    factor_of = block_scale(key, extent, shards, -0.22, 0.18) if shards else 1.0
    drawn = jax.random.normal(key, extent, jnp.float32) * width * factor_of
    return jnp.minimum(jnp.maximum(drawn, -most), most).astype(kind)


def setup_inputs(seed: int = 0) -> dict:
    seeds = jax.random.split(jax.random.key(seed), 20)
    return {
        "tokens": centred(seeds[0], (TOKENS, D), 1.0, 6.0, ((0, 8),)),
        "cotangent": centred(seeds[1], (TOKENS, D), 1.0, 6.0, ((0, 8),)),
        "lengths": draw_lengths(jax.random.fold_in(seeds[19], 71), 0),
        "query_weight": centred(seeds[3], (D, D), D ** -0.5, 0.21875, ((1, 4),)),
        "query_bias": centred(seeds[4], (D,), 0.3, 2.0, ((0, 4),)),
        "key_weight": centred(seeds[5], (D, D), D ** -0.5, 0.21875, ((1, 4),)),
        "key_bias": centred(seeds[6], (D,), 0.3, 2.0, ((0, 4),)),
        "value_weight": centred(seeds[7], (D, D), D ** -0.5, 0.21875, ((1, 4),)),
        "value_bias": centred(seeds[8], (D,), 0.3, 2.0, ((0, 4),)),
        "out_weight": centred(seeds[9], (D, D), (D // 16) ** -0.5, 0.875, ((0, 4),)),
        "out_bias": centred(seeds[10], (D,), 0.3, 2.0),
        "norm_gain": jnp.clip(1.0 + 0.1 * jax.random.normal(seeds[11], (D,), jnp.float32), 0.5, 1.5).astype(jnp.bfloat16),
        "norm_shift": centred(seeds[12], (D,), 0.3, 2.0),
        "up_weight": centred(seeds[13], (D, FF), D ** -0.5, 0.21875, ((1, 4),)),
        "up_bias": centred(seeds[14], (FF,), 0.3, 2.0, ((0, 4),)),
        "down_weight": centred(seeds[15], (FF, D), FF ** -0.5, 0.109375, ((0, 4),)),
        "down_bias": centred(seeds[16], (D,), 0.3, 2.0),
        "final_gain": jnp.clip(1.0 + 0.1 * jax.random.normal(seeds[17], (D,), jnp.float32), 0.5, 1.5).astype(jnp.bfloat16),
        "final_shift": centred(seeds[18], (D,), 0.3, 2.0),
    }


EPSILON = 1e-12
NEG_FILL = -1000000000.0
HIGH = lax.Precision.HIGHEST

@jax.custom_vjp
def low(v):
    return lax.optimization_barrier(v.astype(jnp.bfloat16)).astype(jnp.float32)

@jax.custom_vjp
def low_back(v):
    return v

def low_keep(v):
    return (low(v), None)

def low_pass(kept, grad):
    return (grad,)

def back_keep(v):
    return (v, None)

def back_low(kept, grad):
    return (low(grad),)
low.defvjp(low_keep, low_pass)
low_back.defvjp(back_keep, back_low)

def product(left, right):
    return jnp.dot(left, right, precision=HIGH, preferred_element_type=jnp.float32)

def layout(seq_lengths, count):
    token_place = jnp.arange(count, dtype=jnp.int32)
    seq_ends = jnp.cumsum(seq_lengths).astype(jnp.int32)
    seq_starts = (seq_ends - seq_lengths).astype(jnp.int32)
    segment = lax.optimization_barrier(jnp.sum((token_place[:, None] >= seq_ends[None, :]).astype(jnp.int32), axis=1))
    slot_ids = jnp.arange(seq_lengths.shape[0], dtype=jnp.int32)
    first_place = lax.optimization_barrier(jnp.sum(jnp.where(segment[:, None] == slot_ids[None, :], seq_starts[None, :], 0), axis=1))
    position = (token_place - first_place).astype(jnp.float32)
    live = (token_place < seq_ends[-1]).astype(jnp.float32)
    return (segment, position, live)

def turn_tables(position, head_size):
    frequency = jnp.exp(jnp.arange(head_size // 2, dtype=jnp.float32) * (-2.0 * math.log(10000.0) / head_size))
    angles = position[:, None] * frequency[None, :]
    return (jnp.cos(angles)[:, None, :], jnp.sin(angles)[:, None, :])

def rotate(values, cosine, sine):
    pairs = values.reshape(values.shape[:-1] + (values.shape[-1] // 2, 2))
    even_part = pairs[..., 0]
    odd_part = pairs[..., 1]
    turned = jnp.stack([even_part * cosine - odd_part * sine, even_part * sine + odd_part * cosine], axis=-1)
    return turned.reshape(values.shape)

def normalize(summed, gain, shift):
    centre = summed - lax.optimization_barrier(jnp.mean(summed, axis=-1, keepdims=True))
    spread = lax.optimization_barrier(jnp.mean(centre * centre, axis=-1, keepdims=True))
    return centre * lax.rsqrt(spread + EPSILON) * gain + shift

def forward(tokens, params, segment, cosine, sine, live):
    query_weight, query_bias, key_weight, key_bias, value_weight, value_bias, out_weight, out_bias, norm_gain, norm_shift, up_weight, up_bias, down_weight, down_bias, final_gain, final_shift = params
    count = tokens.shape[0]
    query = low(rotate((low_back(product(tokens, query_weight)) + query_bias).reshape(count, HEADS, HEAD), cosine, sine))
    keys_all = low(rotate((low_back(product(tokens, key_weight)) + key_bias).reshape(count, HEADS, HEAD), cosine, sine))
    values_all = low((low_back(product(tokens, value_weight)) + value_bias).reshape(count, HEADS, HEAD))
    block_rows = min(512, count)
    block_count = count // block_rows

    def attend(pieces):
        query_block, segment_block = pieces
        raw_scores = jnp.einsum('qhd,khd->hqk', query_block, keys_all, precision=HIGH)
        scores = low_back(raw_scores * 0.125)
        same_seq = segment_block[:, None] == segment[None, :]
        scores = jnp.where(same_seq[None], scores, NEG_FILL)
        weights = low(jax.nn.softmax(scores, axis=-1))
        return jnp.einsum('hqk,khd->qhd', weights, values_all, precision=HIGH)
    attended = lax.map(jax.checkpoint(attend), (query.reshape(block_count, block_rows, HEADS, HEAD), segment.reshape(block_count, block_rows)))
    attended = low(low_back(attended.reshape(count, HEADS * HEAD)))
    hidden_one = normalize(tokens + low_back(product(attended, out_weight)) + out_bias, norm_gain, norm_shift)
    pre_act = low_back(product(low(hidden_one), up_weight)) + up_bias
    activated = low(jax.nn.gelu(pre_act, approximate=False))
    second = hidden_one + low_back(product(activated, down_weight)) + down_bias
    return normalize(second, final_gain, final_shift) * live[:, None]

def reference(tokens, cotangent, lengths, query_weight, query_bias, key_weight, key_bias, value_weight, value_bias, out_weight, out_bias, norm_gain, norm_shift, up_weight, up_bias, down_weight, down_bias, final_gain, final_shift):
    params = tuple((weight.astype(jnp.float32) for weight in (query_weight, query_bias, key_weight, key_bias, value_weight, value_bias, out_weight, out_bias, norm_gain, norm_shift, up_weight, up_bias, down_weight, down_bias, final_gain, final_shift)))
    group_tokens_all = tokens.astype(jnp.float32).reshape(GROUPS, CAP, D)
    group_cot_all = cotangent.astype(jnp.float32).reshape(GROUPS, CAP, D)

    def one_group(totals, pieces):
        group_tokens, group_cot, group_lengths = pieces
        segment, position, live = layout(group_lengths, CAP)
        cosine, sine = turn_tables(position, HEAD)
        outcome, pullback = jax.vjp(lambda inputs, weights: forward(inputs, weights, segment, cosine, sine, live), group_tokens, params)
        token_grad, weight_grads = pullback(group_cot)
        totals = jax.tree.map(lambda left, right: left + right, totals, weight_grads)
        return (totals, (outcome.astype(jnp.bfloat16), token_grad))
    zero_grads = jax.tree.map(jnp.zeros_like, params)
    totals, (outputs, token_grads) = lax.scan(one_group, zero_grads, (group_tokens_all, group_cot_all, lengths))
    return (outputs.reshape(TOKENS, D), token_grads.reshape(TOKENS, D), totals[0], totals[1], totals[2], totals[3], totals[4], totals[5], totals[6], totals[7], totals[8], totals[9], totals[10], totals[11], totals[12], totals[13], totals[14], totals[15])
```

```python
import functools
import math

import jax
import jax.numpy as jnp
import numpy as np
from jax import lax
from jax.experimental import pallas as pl
from jax.experimental.pallas import tpu as pltpu
from jax.sharding import PartitionSpec as P

HEAD = 64
HALF = HEAD // 2
WIDE_ROWS = 128
EPSILON = 1e-12
LOG2E = 1.4426950408889634
MASK_FILL = -float(2**30)
SLOT_ROWS = 16
STRIP = 16
VMEM_LIMIT = 56 * 1024 * 1024
LAYER_VMEM_LIMIT = 60 * 1024 * 1024
F32 = jnp.float32
BF16 = jnp.bfloat16


def layout(seq_lengths, count):
    token_place = jnp.arange(count, dtype=jnp.int32)
    seq_ends = jnp.cumsum(seq_lengths)
    seq_starts = seq_ends - seq_lengths
    segment = jnp.sum((token_place[:, None] >= seq_ends[None, :]).astype(jnp.int32), axis=1)
    slot_ids = jnp.arange(seq_lengths.shape[0], dtype=jnp.int32)
    first_place = jnp.sum(
        jnp.where(segment[:, None] == slot_ids[None, :], seq_starts[None, :], 0), axis=1
    )
    position = (token_place - first_place).astype(F32)
    return (segment, position)


def normalize(summed, gain, shift):
    centre = summed - jnp.mean(summed, axis=-1, keepdims=True)
    spread = jnp.mean(centre * centre, axis=-1, keepdims=True)
    return centre * lax.rsqrt(spread + EPSILON) * gain + shift


def dot(left, right, left_dim, right_dim):
    return lax.dot_general(
        left, right, (((left_dim,), (right_dim,)), ((), ())), preferred_element_type=F32
    )


def by_strips(tall, work, *arrays):
    made = []
    for low in range(0, arrays[0].shape[0], tall):
        made.append(work(*[array[low : low + tall] for array in arrays]))
    return [jnp.concatenate(strips, axis=0) for strips in zip(*made)]


def fold_rows(values):
    total = values[:8]
    for low in range(8, values.shape[0], 8):
        total = total + values[low : low + 8]
    return total


def split_pairs(width):
    place = np.zeros((width, width), np.float32)
    for row in range(width):
        head, inner = divmod(row, HEAD)
        half, pair = divmod(inner, HALF)
        place[row, head * HEAD + 2 * pair + half] = 1.0
    return jnp.asarray(place, BF16)


ANY = pl.BlockSpec(memory_space=pl.ANY)


def prepare_kernel(
    place, turn, query_weight, key_weight, value_weight, bias_rows, packed, biases, piece, full
):
    width = turn.shape[0]
    made = 3 * width
    full[:width, :] = dot(turn[...], query_weight[...], 1, 0)
    full[width : 2 * width, :] = dot(turn[...], key_weight[...], 1, 0)
    full[2 * width : made, :] = value_weight[...].astype(F32)
    packed[0] = full[...].astype(BF16)
    biases[0] = jnp.zeros_like(biases[0])
    for index in range(3):
        row = jnp.broadcast_to(bias_rows[0:1, index * width : (index + 1) * width], (8, width))
        if index < 2:
            row = dot(row.astype(BF16), turn[...], 1, 1)
        biases[0, index : index + 1, :width] = row[:1]
    biases[0, 3:4, :] = bias_rows[1:2, :]
    if len(piece.shape) > 1:
        rows = piece.shape[0] - 8
        start = pl.multiple_of(place[0] * rows, 8)
        piece[:rows, :] = full[pl.ds(start, rows), :]
        piece[rows:, :] = biases[0]


def prepare(place, turn, query_weight, key_weight, value_weight, bias_rows, rows):
    width, dim = query_weight.shape
    total = 3 * width
    whole = lambda shape: pl.BlockSpec(shape, lambda i, place: (0,) * len(shape))
    piece = (rows + 8, dim) if rows else (8,)
    return pl.pallas_call(
        prepare_kernel,
        grid_spec=pltpu.PrefetchScalarGridSpec(
            num_scalar_prefetch=1,
            grid=(1,),
            in_specs=[whole((width, width))] + [whole((width, dim))] * 3 + [whole((8, dim))],
            out_specs=[
                whole((1, total, dim)),
                whole((1, 8, dim)),
                whole(piece),
            ],
            scratch_shapes=[pltpu.VMEM((total, dim), F32)],
        ),
        out_shape=[
            jax.ShapeDtypeStruct((1, total, dim), BF16),
            jax.ShapeDtypeStruct((1, 8, dim), F32),
            jax.ShapeDtypeStruct(piece, F32),
        ],
        compiler_params=pltpu.CompilerParams(vmem_limit_bytes=VMEM_LIMIT),
        name="prepare",
    )(place, turn, query_weight, key_weight, value_weight, bias_rows)


def cut_kernel(place, up, down, out, *refs):
    piece, full = refs[-2], refs[-1]
    rows = up.shape[0]
    piece[:rows, :] = up[...].astype(F32)
    piece[rows : 2 * rows, :] = down[...].astype(F32)
    few = piece.shape[0] - 2 * rows
    full[...] = out[...].astype(F32)
    piece[2 * rows :, :] = full[pl.ds(pl.multiple_of(place[0] * few, 8), few), :]


def cut_pieces(place, up, down, out, rows, few, after):
    dim = up.shape[1]
    here = lambda rows: pl.BlockSpec((rows, dim), lambda i, place: (place[0], 0))
    return pl.pallas_call(
        cut_kernel,
        grid_spec=pltpu.PrefetchScalarGridSpec(
            num_scalar_prefetch=1,
            grid=(1,),
            in_specs=[here(rows), here(rows), pl.BlockSpec(out.shape, lambda i, place: (0, 0))]
            + [ANY] * len(after),
            out_specs=pl.BlockSpec((2 * rows + few, dim), lambda i, place: (0, 0)),
            scratch_shapes=[pltpu.VMEM(out.shape, F32)],
        ),
        out_shape=jax.ShapeDtypeStruct((2 * rows + few, dim), F32),
        name="cut_pieces",
    )(place, up, down, out, *after)


def stack_kernel(count, *refs):
    pieces, mine, extra = refs[:count], refs[-2], refs[-1]
    rows = mine.shape[1]
    for index, piece in enumerate(pieces):
        mine[index] = piece[:rows, :]
        extra[index] = piece[rows:, :]


def stack_pieces(pieces, rows, after):
    tall, dim = pieces[0].shape
    count = len(pieces)
    vmem = pl.BlockSpec(memory_space=pltpu.VMEM)
    return pl.pallas_call(
        functools.partial(stack_kernel, count),
        in_specs=[vmem] * count + [ANY] * len(after),
        out_specs=[vmem, vmem],
        out_shape=[
            jax.ShapeDtypeStruct((count, rows, dim), F32),
            jax.ShapeDtypeStruct((count, tall - rows, dim), F32),
        ],
        compiler_params=pltpu.CompilerParams(vmem_limit_bytes=VMEM_LIMIT),
        name="stack_pieces",
    )(*pieces, *after)


def turn_kernel(own, gathered, *refs):
    refs[-1][...] = gathered[...]


def turn_pieces(own, gathered, after):
    shards, rows, dim = gathered.shape
    return pl.pallas_call(
        turn_kernel,
        grid_spec=pltpu.PrefetchScalarGridSpec(
            num_scalar_prefetch=1,
            grid=(shards - 1,),
            in_specs=[
                pl.BlockSpec((1, rows, dim), lambda j, own: ((own[0] + 1 + j) % shards, 0, 0))
            ]
            + [ANY] * len(after),
            out_specs=pl.BlockSpec((1, rows, dim), lambda j, own: (j, 0, 0)),
        ),
        out_shape=jax.ShapeDtypeStruct((shards - 1, rows, dim), F32),
        compiler_params=pltpu.CompilerParams(vmem_limit_bytes=VMEM_LIMIT),
        name="turn_pieces",
    )(own, gathered, *after)


def halve_kernel(side, ahead, *refs):
    upper, lower = refs[-2:]
    cut_row = upper.shape[1]
    upper[...] = side[:, :cut_row, :]
    lower[...] = ahead[:, cut_row:, :]


def halve_pieces(side, ahead, cut_row, after):
    count, rows, dim = side.shape
    vmem = pl.BlockSpec(memory_space=pltpu.VMEM)
    return pl.pallas_call(
        halve_kernel,
        in_specs=[vmem, vmem] + [ANY] * len(after),
        out_specs=[vmem, vmem],
        out_shape=[
            jax.ShapeDtypeStruct((count, cut_row, dim), F32),
            jax.ShapeDtypeStruct((count, rows - cut_row, dim), F32),
        ],
        compiler_params=pltpu.CompilerParams(vmem_limit_bytes=VMEM_LIMIT),
        name="halve_pieces",
    )(side, ahead, *after)


def join_kernel(upper, lower, *refs):
    joined = refs[-1]
    cut_row = upper.shape[1]
    joined[:, :cut_row, :] = upper[...]
    joined[:, cut_row:, :] = lower[...]


def join_pieces(upper, lower, after):
    count, cut_row, dim = upper.shape
    vmem = pl.BlockSpec(memory_space=pltpu.VMEM)
    return pl.pallas_call(
        join_kernel,
        in_specs=[vmem, vmem] + [ANY] * len(after),
        out_specs=vmem,
        out_shape=jax.ShapeDtypeStruct((count, cut_row + lower.shape[1], dim), F32),
        compiler_params=pltpu.CompilerParams(vmem_limit_bytes=VMEM_LIMIT),
        name="join_pieces",
    )(upper, lower, *after)


def start_copies(places, parts, begins, shard, first, size, target, sems):
    copies = []
    for index, (part, begin) in enumerate(zip(parts, begins)):
        low, high = max(first, begin), min(first + size, begin + part.shape[1])
        if low >= high:
            continue
        start = pl.multiple_of(places[index] * size + (low - first), 8)
        copy = pltpu.make_async_copy(
            part.at[shard, pl.ds(low - begin, high - low), :],
            target.at[pl.ds(start, high - low), :],
            sems.at[index],
        )
        copy.start()
        copies.append(copy)
    return copies


def project_kernel(begins, size, places, tokens, cosine, sine, slots, biases, *refs):
    count_parts = len(begins)
    query_t, key_n, key_t, value_t, value_n = refs[-8:-3] if count_parts else refs[-6:-1]
    heads = query_t.shape[0]
    width = heads * HEAD
    if count_parts:
        tokens_t = tokens[...]
    else:
        tokens_t = tokens[...].T
        refs[-1][...] = tokens_t
    count = tokens_t.shape[1]
    if count_parts:
        parts, packed = refs[:count_parts], refs[-3]
        stage, sems = refs[-2], refs[-1]

        @pl.when(pl.program_id(1) == 0)
        def _():
            shard = pl.program_id(0)
            for copy in start_copies(places, parts, begins, shard, 0, size, stage, sems):
                copy.wait()
            packed[0] = stage[...].astype(BF16)

    else:
        packed = refs[0]

    bias = biases[0].T[:width, :]
    bias = jnp.concatenate([bias[:, 0:1], bias[:, 1:2], bias[:, 2:3]], axis=0)
    made = dot(packed[0], tokens_t, 1, 0) + bias
    cos, sin = cosine[...], sine[...]
    same = slots[...]
    same_low = same.astype(BF16)
    row = lax.broadcasted_iota(jnp.int32, (HEAD, count), 0)
    mask_rows = (1.0 - same) * MASK_FILL
    key_mask = jnp.concatenate(
        [mask_rows, jnp.zeros((HEAD - SLOT_ROWS, count), F32)], axis=0
    ).astype(BF16)
    value_ones = jnp.where(row < 2, 1.0, 0.0).astype(BF16)
    row16 = lax.broadcasted_iota(jnp.int32, (16, count), 0)
    ones16 = jnp.where(row16 < 1, 1.0, 0.0).astype(BF16)

    def rotate(rows):
        even, odd = rows[:HALF], rows[HALF:]
        return jnp.concatenate([even * cos - odd * sin, even * sin + odd * cos], axis=0)

    for head in range(heads):
        low = head * HEAD
        query = rotate(made[low : low + HEAD]) * (0.125 * LOG2E)
        query_t[head, :HEAD, :] = query.astype(BF16)
        query_t[head, HEAD : HEAD + SLOT_ROWS, :] = same_low
        query_t[head, HEAD + SLOT_ROWS :, :] = jnp.zeros(
            (WIDE_ROWS - HEAD - SLOT_ROWS, count), BF16
        )
        key = rotate(made[width + low : width + low + HEAD]).astype(BF16)
        key_t[head] = key
        key_n[head] = jnp.concatenate([key, key_mask], axis=0).T
        value = made[2 * width + low : 2 * width + low + HEAD].astype(BF16)
        value_t[head, :HEAD, :] = value
        value_t[head, HEAD:, :] = ones16
        value_n[head] = jnp.concatenate([value, value_ones], axis=0).T


def project(places, parts, begins, size, packed, biases, tokens, cosine, sine, slots, heads, after):
    dim, count = tokens.shape if parts else tokens.shape[::-1]
    shards = biases.shape[0]
    block = min(1024, count)
    total = shards * heads
    token_block = pl.BlockSpec((dim, block), lambda j, i, ids: (0, i))
    rows = 3 * heads * HEAD
    shard_block = pl.BlockSpec((1, rows, dim), lambda j, i, ids: (j, 0, 0))
    spec = pltpu.PrefetchScalarGridSpec(
        num_scalar_prefetch=1,
        grid=(shards, count // block),
        in_specs=[
            token_block if parts else pl.BlockSpec((block, dim), lambda j, i, ids: (i, 0)),
            pl.BlockSpec((HALF, block), lambda j, i, ids: (0, i)),
            pl.BlockSpec((HALF, block), lambda j, i, ids: (0, i)),
            pl.BlockSpec((SLOT_ROWS, block), lambda j, i, ids: (0, i)),
            pl.BlockSpec((1, 8, dim), lambda j, i, ids: (j, 0, 0)),
        ]
        + ([ANY] * len(parts) if parts else [shard_block])
        + [ANY] * len(after),
        out_specs=[
            pl.BlockSpec((heads, WIDE_ROWS, block), lambda j, i, ids: (j, 0, i)),
            pl.BlockSpec((heads, block, WIDE_ROWS), lambda j, i, ids: (j, i, 0)),
            pl.BlockSpec((heads, HEAD, block), lambda j, i, ids: (j, 0, i)),
            pl.BlockSpec((heads, HEAD + 16, block), lambda j, i, ids: (j, 0, i)),
            pl.BlockSpec((heads, block, WIDE_ROWS), lambda j, i, ids: (j, i, 0)),
        ]
        + [shard_block if parts else token_block],
        scratch_shapes=[
            pltpu.VMEM((rows, dim), F32),
            pltpu.SemaphoreType.DMA((len(parts),)),
        ]
        if parts
        else [],
    )
    return pl.pallas_call(
        functools.partial(project_kernel, tuple(begins), size),
        grid_spec=spec,
        out_shape=[
            jax.ShapeDtypeStruct((total, WIDE_ROWS, count), BF16),
            jax.ShapeDtypeStruct((total, count, WIDE_ROWS), BF16),
            jax.ShapeDtypeStruct((total, HEAD, count), BF16),
            jax.ShapeDtypeStruct((total, HEAD + 16, count), BF16),
            jax.ShapeDtypeStruct((total, count, WIDE_ROWS), BF16),
        ]
        + [jax.ShapeDtypeStruct((shards, rows, dim) if parts else (dim, count), BF16)],
        compiler_params=pltpu.CompilerParams(vmem_limit_bytes=VMEM_LIMIT),
        name="project",
    )(places, tokens, cosine, sine, slots, biases, *(parts or [packed]), *after)


def attend_kernel(key_n, query_t, value_t, *refs):
    probs_t, out_low, out_full, inverse, even_scores, odd_scores, even_peak, odd_peak = refs[-8:]
    count = key_n.shape[1]
    width = query_t.shape[2]
    chunk = min(256, count)

    def run(new_scores, new_peak, scores, peak_ref):
        query = query_t[0]
        last_peak = jnp.broadcast_to(peak_ref[...], (STRIP, width))
        peak = None
        total = jnp.zeros((HEAD + 16, width), F32)
        for low in range(0, count, chunk):
            part = dot(key_n[0, low : low + chunk, :], query, 1, 0)
            raised = []
            for row in range(low, low + chunk, STRIP):
                strip = part[row - low : row - low + STRIP]
                new_scores[row : row + STRIP, :] = strip
                peak = strip if peak is None else jnp.maximum(peak, strip)
                strip = jnp.exp2(scores[row : row + STRIP, :] - last_peak).astype(BF16)
                probs_t[0, 0, row : row + STRIP, :] = strip
                raised.append(strip)
            raised = jnp.concatenate(raised, axis=0)
            total = total + dot(value_t[0, :, low : low + chunk], raised, 1, 0)
        new_peak[...] = jnp.max(peak, axis=0, keepdims=True)
        scale = 1.0 / total[HEAD : HEAD + 1, :]
        inverse[0] = scale
        out = total[:HEAD, :] * scale
        out_full[...] = out
        out_low[...] = out.astype(BF16)

    odd = lax.rem(pl.program_id(0), 2)

    @pl.when(odd == 0)
    def _():
        run(even_scores, even_peak, odd_scores, odd_peak)

    @pl.when(odd == 1)
    def _():
        run(odd_scores, odd_peak, even_scores, even_peak)


def attend(made, first, number, into, after):
    query_t, key_n, _, value_t, _ = made[:5]
    total, count, _ = key_n.shape
    width = min(1024, count)
    steps = count // width
    last = number * steps - 1
    now = lambda s: jnp.minimum(s, last)
    past = lambda s: jnp.maximum(s - 1, 0)
    head_now = lambda s: first + now(s) // steps
    head_past = lambda s: first + past(s) // steps
    into = list(into)
    return pl.pallas_call(
        attend_kernel,
        grid=(number * steps + 1,),
        in_specs=[
            pl.BlockSpec((1, count, WIDE_ROWS), lambda s: (head_now(s), 0, 0)),
            pl.BlockSpec((1, WIDE_ROWS, width), lambda s: (head_now(s), 0, now(s) % steps)),
            pl.BlockSpec((1, HEAD + 16, count), lambda s: (head_past(s), 0, 0)),
        ]
        + [ANY] * (len(into) + len(after)),
        out_specs=[
            pl.BlockSpec((1, 1, count, width), lambda s: (head_past(s), past(s) % steps, 0, 0)),
            pl.BlockSpec((HEAD, width), lambda s: (head_past(s), past(s) % steps)),
            pl.BlockSpec((HEAD, width), lambda s: (head_past(s), past(s) % steps)),
            pl.BlockSpec((1, 1, width), lambda s: (head_past(s), 0, past(s) % steps)),
        ],
        out_shape=[
            jax.ShapeDtypeStruct((total, steps, count, width), BF16),
            jax.ShapeDtypeStruct((total * HEAD, count), BF16),
            jax.ShapeDtypeStruct((total * HEAD, count), F32),
            jax.ShapeDtypeStruct((total, 1, count), F32),
        ],
        scratch_shapes=[
            pltpu.VMEM((count, width), F32),
            pltpu.VMEM((count, width), F32),
            pltpu.VMEM((1, width), F32),
            pltpu.VMEM((1, width), F32),
        ],
        input_output_aliases={3 + index: index for index in range(len(into))},
        compiler_params=pltpu.CompilerParams(vmem_limit_bytes=VMEM_LIMIT),
        name="attend",
    )(key_n, query_t, value_t, *into, *after)


def gelu_parts(inner):
    size = jnp.abs(inner)
    fall = jnp.exp2(inner * inner * (-0.5 * LOG2E))
    base = 1.0 + (0.3275911 * math.sqrt(0.5)) * size
    ratio = pl.reciprocal(base, approx=True)
    ratio = ratio * (2.0 - base * ratio)
    tail = 0.5 * 1.061405429 * ratio - 0.5 * 1.453152027
    tail = tail * ratio + 0.5 * 1.421413741
    tail = tail * ratio - 0.5 * 0.284496736
    tail = tail * ratio + 0.5 * 0.254829592
    tail = tail * ratio * fall
    share = jnp.where(inner < 0.0, tail, 1.0 - tail)
    density = fall * (1.0 / math.sqrt(2.0 * math.pi))
    return (inner * share).astype(BF16), (share + inner * density).astype(BF16)


def layer_kernel(
    groups,
    begins,
    sizes,
    places,
    ends,
    tokens,
    cotangent,
    vectors,
    biases_own,
    biases_rest,
    out_own,
    up_own,
    down_own,
    *refs,
):
    attended, refs = refs[: len(groups)], refs[len(groups) :]
    parts, refs = refs[: len(begins)], refs[len(begins) :]
    layer_out, summed_grad_ref, up_grad, down_grad, out_grad, small = refs[:6]
    attended_grads, refs = refs[6 : 6 + len(groups)], refs[6 + len(groups) :]
    (
        up_all,
        down_all,
        out_all,
        slopes,
        stage,
        up_sum,
        down_sum,
        sums,
        sems,
        out_sems,
    ) = refs
    step = pl.program_id(0)
    count, dim = tokens.shape
    shards = up_all.shape[0]
    width = out_own.shape[0]
    streams = 2
    rows = count // streams

    @pl.when(step == 0)
    def _():
        sums[...] = jnp.zeros_like(sums)
        up_sum[...] = jnp.zeros_like(up_sum)
        down_sum[...] = jnp.zeros_like(down_sum)
        out_grad[...] = jnp.zeros_like(out_grad)
        jobs = [
            (kind, target, shard)
            for shard in range(shards - 1)
            for kind, target in ((2, out_all), (0, up_all), (1, down_all))
        ]
        slots = stage.shape[0]

        def begin(number):
            kind, target, shard = jobs[number]
            slot = number % slots
            first = sum(sizes[:kind])
            return start_copies(
                places, parts, begins, shard, first, sizes[kind], stage.at[slot], sems.at[slot]
            )

        running = [begin(number) for number in range(slots)]
        up_all[0] = up_own[...]
        down_all[0] = down_own[...]
        out_all[0] = out_own[...]
        for number, (_, target, shard) in enumerate(jobs):
            for copy in running.pop(0):
                copy.wait()
            tall = target.shape[1]
            target[shard + 1] = stage[number % slots, :tall, :].astype(BF16)
            if number + slots < len(jobs):
                running.append(begin(number + slots))

    def mean(values):
        return jnp.sum(values, axis=-1, keepdims=True) * (1.0 / dim)

    out_bias, norm_gain, norm_shift = vectors[0:1, :], vectors[1:2, :], vectors[2:3, :]
    down_bias, final_gain, final_shift = vectors[3:4, :], vectors[4:5, :], vectors[5:6, :]
    hidden_biases = [biases_own[0, 3:4, :]]
    hidden_biases += [biases_rest[index, 3:4, :] for index in range(shards - 1)]
    where = [(group, part) for group, size in enumerate(groups) for part in range(size)]

    def fold(index, values):
        sums[index] += jnp.sum(values.reshape(rows // 8, 8, values.shape[1]), axis=0)

    def stream(low):
        here = slice(low, low + rows)
        total = tokens[here, :].astype(F32) + out_bias
        for shard, (group, part) in enumerate(where):
            seen = attended[group][part * width : (part + 1) * width, here]
            total = total + dot(seen, out_all[shard], 0, 0)
        yield
        centre = total - mean(total)
        norm_scale = lax.rsqrt(mean(centre * centre) + EPSILON)
        normal = centre * norm_scale
        hidden = normal * norm_gain + norm_shift
        hidden_low = hidden.astype(BF16)
        second = hidden + down_bias
        yield
        inner = dot(hidden_low, up_all[0], 1, 0) + hidden_biases[0]
        yield
        own_active = None
        for shard in range(shards):
            active, slope = gelu_parts(inner)
            slopes[shard, here, :] = slope
            if shard == 0:
                own_active = active
            yield
            if shard + 1 < shards:
                inner = dot(hidden_low, up_all[shard + 1], 1, 0) + hidden_biases[shard + 1]
            second = second + dot(active, down_all[shard], 1, 0)
            yield
        centre = second - mean(second)
        final_scale = lax.rsqrt(mean(centre * centre) + EPSILON)
        final = centre * final_scale
        token = step * count + low + lax.broadcasted_iota(jnp.int32, (rows, 1), 0)
        alive = jnp.where(token < ends[0], 1.0, 0.0)
        layer_out[here, :] = ((final * final_gain + final_shift) * alive).astype(BF16)
        grad = cotangent[here, :].astype(F32) * alive
        fold(2, grad * final)
        fold(3, grad)
        scaled = grad * final_gain
        second_grad = final_scale * (scaled - mean(scaled) - final * mean(scaled * final))
        fold(1, second_grad)
        second_low = second_grad.astype(BF16)
        yield
        hidden_grad = second_grad
        following = dot(second_low, down_all[0], 1, 1)
        down_sum[...] += dot(own_active, second_low, 0, 0)
        yield
        for shard in range(shards):
            inner_grad = following * slopes[shard, here, :].astype(F32)
            inner_low = inner_grad.astype(BF16)
            if shard == 0:
                fold(0, inner_grad)
            yield
            if shard + 1 < shards:
                following = dot(second_low, down_all[shard + 1], 1, 1)
            if shard == 0:
                up_sum[...] += dot(hidden_low, inner_low, 0, 0)
            hidden_grad = hidden_grad + dot(inner_low, up_all[shard], 1, 1)
            yield
        fold(4, hidden_grad * normal)
        fold(5, hidden_grad)
        scaled = hidden_grad * norm_gain
        summed_grad = norm_scale * (scaled - mean(scaled) - normal * mean(scaled * normal))
        fold(6, summed_grad)
        summed_grad_ref[here, :] = summed_grad
        summed_low = summed_grad.astype(BF16)
        yield
        out_grad[...] += dot(attended[0][:, here], summed_low, 1, 0)
        for shard, (group, part) in enumerate(where):
            attended_grads[group][part * width : (part + 1) * width, here] = dot(
                out_all[shard], summed_low, 1, 1
            )
        yield

    running = [stream(index * rows) for index in range(streams)]
    next(running[0])
    while running:
        for work in list(reversed(running)):
            try:
                next(work)
            except StopIteration:
                running.remove(work)

    @pl.when(step == pl.num_programs(0) - 1)
    def _():
        copies = [
            pltpu.make_async_copy(up_sum, up_grad, out_sems.at[0]),
            pltpu.make_async_copy(down_sum, down_grad, out_sems.at[1]),
        ]
        for copy in copies:
            copy.start()
        for index in range(7):
            small[index : index + 1, :] = jnp.sum(sums[index], axis=0, keepdims=True)
        small[7:8, :] = jnp.zeros((1, dim), F32)
        for copy in copies:
            copy.wait()


def layer(
    places,
    ends,
    attended,
    tokens,
    cotangent,
    vectors,
    biases,
    out_own,
    up_own,
    down_own,
    parts,
    begins,
    sizes,
):
    count, dim = tokens.shape
    width = out_own.shape[0]
    groups = tuple(seen.shape[0] // width for seen in attended)
    shards = sum(groups)
    hidden = up_own.shape[1]
    block = min(512, count)
    whole = lambda shape: pl.BlockSpec(shape, lambda i, *_: (0,) * len(shape))
    rowed = pl.BlockSpec((block, dim), lambda i, *_: (i, 0))
    columns = [pl.BlockSpec((size * width, block), lambda i, *_: (0, i)) for size in groups]
    far = pl.BlockSpec(memory_space=pltpu.HBM)
    spec = pltpu.PrefetchScalarGridSpec(
        num_scalar_prefetch=2,
        grid=(count // block,),
        in_specs=[rowed, rowed, whole((8, dim))]
        + [whole(bias.shape) for bias in biases]
        + [whole((width, dim)), whole((dim, hidden)), whole((hidden, dim))]
        + columns
        + [ANY] * len(parts),
        out_specs=[rowed, rowed, far, far, whole((width, dim)), whole((8, dim))] + columns,
        scratch_shapes=[
            pltpu.VMEM((shards, dim, hidden), BF16),
            pltpu.VMEM((shards, hidden, dim), BF16),
            pltpu.VMEM((shards, width, dim), BF16),
            pltpu.VMEM((shards, block, hidden), BF16),
            pltpu.VMEM((3, max(dim, hidden), dim), F32),
            pltpu.VMEM((dim, hidden), F32),
            pltpu.VMEM((hidden, dim), F32),
            pltpu.VMEM((7, 8, dim), F32),
            pltpu.SemaphoreType.DMA((3, len(parts))),
            pltpu.SemaphoreType.DMA((2,)),
        ],
    )
    return pl.pallas_call(
        functools.partial(layer_kernel, groups, tuple(begins), tuple(sizes)),
        grid_spec=spec,
        out_shape=[
            jax.ShapeDtypeStruct((count, dim), BF16),
            jax.ShapeDtypeStruct((count, dim), F32),
            jax.ShapeDtypeStruct((dim, hidden), F32),
            jax.ShapeDtypeStruct((hidden, dim), F32),
            jax.ShapeDtypeStruct((width, dim), F32),
            jax.ShapeDtypeStruct((8, dim), F32),
        ]
        + [jax.ShapeDtypeStruct(seen.shape, F32) for seen in attended],
        compiler_params=pltpu.CompilerParams(vmem_limit_bytes=LAYER_VMEM_LIMIT),
        name="layer",
    )(
        places,
        ends,
        tokens,
        cotangent,
        vectors,
        *biases,
        out_own,
        up_own,
        down_own,
        *attended,
        *parts,
    )


def own_grads_kernel(
    turn, back, tokens, out_grad, small, sums, query_grad, key_grad, value_grad, tail
):
    width, dim = out_grad.shape
    query_grad[...] = dot(dot(turn[...], back[0, 0], 0, 0).astype(BF16), tokens[...], 1, 0)
    key_grad[...] = dot(dot(turn[...], back[0, 1], 0, 0).astype(BF16), tokens[...], 1, 0)
    value_grad[...] = dot(back[0, 2], tokens[...], 1, 0)
    tail[:width, :] = out_grad[...]
    tail[width : width + 8, :] = small[...]
    tail[width + 8 :, :] = jnp.zeros((tail.shape[0] - width - 8, dim), F32)
    turned = turn[...].astype(F32)
    for index in range(3):
        row = jnp.sum(sums[0, index].T, axis=0, keepdims=True)
        if index < 2:
            row = lax.dot_general(
                jnp.broadcast_to(row, (8, width)),
                turned,
                (((1,), (0,)), ((), ())),
                precision=lax.Precision.HIGHEST,
                preferred_element_type=F32,
            )[:1]
        tail[width + 8 + index : width + 9 + index, :width] = row


def own_grads(turn, back, tokens, out_grad, small, sums):
    dim, width = tokens.shape[1], turn.shape[0]
    return pl.pallas_call(
        own_grads_kernel,
        out_shape=[jax.ShapeDtypeStruct((width, dim), F32)] * 3
        + [jax.ShapeDtypeStruct((width + 16, dim), F32)],
        compiler_params=pltpu.CompilerParams(vmem_limit_bytes=VMEM_LIMIT),
        name="own_grads",
    )(turn, back, tokens, out_grad, small, sums)


def tokens_kernel(groups, summed_grad, *refs):
    backs, packed, out = refs[: len(groups)], refs[len(groups) : -1], refs[-1]
    total = summed_grad[...]
    for back, weights, size in zip(backs, packed, groups):
        rows = weights.shape[1]
        for shard in range(size):
            total = total + dot(back[shard * rows : (shard + 1) * rows, :], weights[shard], 0, 0)
    out[...] = total


def tokens_back(summed_grad, backs, packed):
    count, dim = summed_grad.shape
    groups = tuple(weights.shape[0] for weights in packed)
    block = min(512, count)
    rowed = pl.BlockSpec((block, dim), lambda i: (i, 0))
    return pl.pallas_call(
        functools.partial(tokens_kernel, groups),
        grid=(count // block,),
        in_specs=[rowed]
        + [pl.BlockSpec((back.shape[0], block), lambda i: (0, i)) for back in backs]
        + [pl.BlockSpec(weights.shape, lambda i: (0, 0, 0)) for weights in packed],
        out_specs=rowed,
        out_shape=jax.ShapeDtypeStruct((count, dim), F32),
        compiler_params=pltpu.CompilerParams(vmem_limit_bytes=VMEM_LIMIT),
        name="tokens_back",
    )(summed_grad, *backs, *packed)


def attend_back_kernel(
    probs_t,
    value_n,
    key_t,
    query_t,
    out_full,
    out_grad,
    inverse,
    cosine,
    sine,
    back,
    sums,
    both_total,
):
    step = pl.program_id(1)
    count = value_n.shape[1]
    width = query_t.shape[2]
    chunk = min(256, count)

    @pl.when(step == 0)
    def _():
        both_total[...] = jnp.zeros_like(both_total)
        sums[...] = jnp.zeros_like(sums)

    grad = (out_grad[...] * inverse[0]).astype(BF16)
    inner = jnp.sum(grad.astype(F32) * out_full[...], axis=0, keepdims=True)
    inner_high = inner.astype(BF16)
    inner_low = (inner - inner_high.astype(F32)).astype(BF16)
    row = lax.broadcasted_iota(jnp.int32, (16, width), 0)
    tail = jnp.where(
        row == 0,
        -inner_high.astype(F32),
        jnp.where(row == 1, -inner_low.astype(F32), 0.0),
    ).astype(BF16)
    grad_wide = jnp.concatenate(
        [grad, tail, jnp.zeros((WIDE_ROWS - HEAD - 16, width), BF16)], axis=0
    )
    query = query_t[0, :HEAD, :]
    nothing = jnp.zeros((HEAD, width), BF16)
    grad_left = jnp.concatenate([grad, nothing], axis=0).T
    query_right = jnp.concatenate([nothing, query], axis=0).T
    query_total = jnp.zeros((HEAD, width), F32)
    changed = lambda low: dot(value_n[0, low : low + chunk, :], grad_wide, 1, 0)
    following = changed(0)
    for low in range(0, count, chunk):
        change = following
        if low + chunk < count:
            following = changed(low + chunk)
        weights = probs_t[0, 0, low : low + chunk, :]
        (score,) = by_strips(
            STRIP, lambda seen, other: ((seen.astype(F32) * other).astype(BF16),), weights, change
        )
        both_total[low : low + chunk, :] += dot(weights, grad_left, 1, 0) + dot(
            score, query_right, 1, 0
        )
        query_total = query_total + dot(key_t[0, :, low : low + chunk], score, 1, 0)

    def unrotate(rows, cos, sin):
        even, odd = rows[:HALF], rows[HALF:]
        return jnp.concatenate([even * cos + odd * sin, odd * cos - even * sin], axis=0)

    def fold(rows):
        total = rows[:, :128]
        for low in range(128, rows.shape[1], 128):
            total = total + rows[:, low : low + 128]
        return total

    here = pl.ds(pl.multiple_of(step * width, width), width)
    query_back = unrotate(query_total * 0.125, cosine[:, here], sine[:, here])
    back[0, 0, :, here] = query_back.astype(BF16)
    sums[0, 0] += fold(query_back)

    @pl.when(step == pl.num_programs(1) - 1)
    def _():
        both = both_total[...].T
        key_back = unrotate(both[HEAD:] * (1.0 / LOG2E), cosine[...], sine[...])
        back[0, 1] = key_back.astype(BF16)
        sums[0, 1] = fold(key_back)
        value_back = both[:HEAD]
        back[0, 2] = value_back.astype(BF16)
        sums[0, 2] = fold(value_back)


def attend_back(probs_t, value_n, key_t, query_t, out_full, out_grad, inverse, cosine, sine, heads):
    total, steps, count, width = probs_t.shape
    shards = total // heads
    place = lambda h, i: (h // heads, 0, h % heads, 0)
    return pl.pallas_call(
        attend_back_kernel,
        grid=(total, steps),
        in_specs=[
            pl.BlockSpec((1, 1, count, width), lambda h, i: (h, i, 0, 0)),
            pl.BlockSpec((1, count, WIDE_ROWS), lambda h, i: (h, 0, 0)),
            pl.BlockSpec((1, HEAD, count), lambda h, i: (h, 0, 0)),
            pl.BlockSpec((1, WIDE_ROWS, width), lambda h, i: (h, 0, i)),
            pl.BlockSpec((HEAD, width), lambda h, i: (h, i)),
            pl.BlockSpec((HEAD, width), lambda h, i: (h, i)),
            pl.BlockSpec((1, 1, width), lambda h, i: (h, 0, i)),
            pl.BlockSpec((HALF, count), lambda h, i: (0, 0)),
            pl.BlockSpec((HALF, count), lambda h, i: (0, 0)),
        ],
        out_specs=[
            pl.BlockSpec((1, 3, HEAD, count), place),
            pl.BlockSpec((1, 3, HEAD, 128), place),
        ],
        out_shape=[
            jax.ShapeDtypeStruct((shards, 3, heads * HEAD, count), BF16),
            jax.ShapeDtypeStruct((shards, 3, heads * HEAD, 128), F32),
        ],
        scratch_shapes=[pltpu.VMEM((count, 2 * HEAD), F32)],
        compiler_params=pltpu.CompilerParams(vmem_limit_bytes=VMEM_LIMIT),
        name="attend_back",
    )(probs_t, value_n, key_t, query_t, out_full, out_grad, inverse, cosine, sine)


def body(
    tokens,
    cotangent,
    lengths,
    query_weight,
    query_bias,
    key_weight,
    key_bias,
    value_weight,
    value_bias,
    out_weight,
    out_bias,
    norm_gain,
    norm_shift,
    up_weight,
    up_bias,
    down_weight,
    down_bias,
    final_gain,
    final_shift,
):
    count, dim = tokens.shape
    width = query_weight.shape[1]
    heads = width // HEAD
    narrow = lax.axis_size("narrow")
    wide = lax.axis_size("wide")
    place = lax.axis_index("wide")
    segment, position = layout(lengths[0], count)
    frequency = jnp.exp(
        jnp.arange(HALF, dtype=F32) * (-2.0 * math.log(10000.0) / HEAD)
    )
    angles = frequency[:, None] * position[None, :]
    cosine, sine = jnp.cos(angles), jnp.sin(angles)
    slots = (segment[None, :] == jnp.arange(SLOT_ROWS, dtype=jnp.int32)[:, None]).astype(F32)

    turn = split_pairs(width)
    empty = lambda number: jnp.zeros((number,), BF16)
    bias_rows = jnp.concatenate(
        [query_bias, key_bias, value_bias, empty(-3 * width % dim), up_bias, empty(6 * dim)]
    )
    bias_rows = bias_rows.astype(F32).reshape(8, dim)
    vectors = jnp.concatenate(
        [out_bias, norm_gain, norm_shift, down_bias, final_gain, final_shift, empty(2 * dim)]
    )
    vectors = vectors.astype(F32).reshape(8, dim)
    ends = jnp.sum(lengths[0]).astype(jnp.int32).reshape(1)
    permuted = wide == 8 and narrow == 4
    made = 3 * width
    slice_rows = made // wide if permuted else 0
    place_ref = place.astype(jnp.int32).reshape(1)
    packed_own, biases_own, attn_piece = prepare(
        place_ref, turn, query_weight.T, key_weight.T, value_weight.T, bias_rows, slice_rows
    )

    def shift(value, distance):
        moves = [((shard + distance) % narrow, shard) for shard in range(narrow)]
        return lax.ppermute(value, "narrow", moves)

    def flip(value, mask):
        return lax.ppermute(value, "wide", [(index, index ^ mask) for index in range(wide)])

    def gathered(block, distances):
        size = block.shape[0] // wide
        piece = lax.dynamic_slice_in_dim(block, place * size, size, axis=0).astype(F32)
        pieces = jnp.stack([shift(piece, distance) for distance in distances])
        return lax.all_gather(pieces, "wide", axis=1, tiled=True)

    def scattered(masks):
        return jnp.stack([place ^ mask for mask in masks]).astype(jnp.int32)

    nowhere = jnp.zeros((1,), jnp.int32)
    own = project(
        nowhere, [], (), 0, packed_own, biases_own, tokens, cosine, sine, slots, heads, []
    )
    own_seen = attend(own, 0, 1, [], [])
    masks = (0, 2, 4, 6, 6, 1, 3, 5, 7, 7)
    if permuted:
        sizes = (up_weight.shape[0] // wide, down_weight.shape[0] // wide, width // wide)
        cut_row = (slice_rows // 2 + 7) // 8 * 8
        mine, biases_rest = stack_pieces(
            [shift(attn_piece, distance) for distance in range(1, narrow)],
            slice_rows,
            [own_seen[3]],
        )
        side, ahead, core_mine = flip(mine, 2), flip(mine, 4), flip(mine, 1)
        layer_piece = cut_pieces(
            place_ref, up_weight, down_weight, out_weight, sizes[0], sizes[2], [mine]
        )
        layer_pieces = lax.all_gather(layer_piece, "narrow", axis=0)
        own_seen = attend(own, 1, heads - 1, own_seen, [layer_piece])
        upper, lower = halve_pieces(side, ahead, cut_row, [own_seen[3]])
        across = [flip(upper, 4), flip(lower, 2)]
        core = [core_mine, flip(side, 1), flip(ahead, 1)] + [flip(value, 1) for value in across]
        rest_parts = [mine, side, ahead] + across + core
        rest_begins = (0, 0, 0, 0, cut_row, 0, 0, 0, 0, cut_row)
        rest_places, rest_size = scattered(masks), slice_rows
    else:
        own_seen = attend(own, 1, heads - 1, own_seen, [])
        rest_parts = [gathered(packed_own[0], range(1, narrow))]
        biases_rest = jnp.stack([shift(biases_own[0], step) for step in range(1, narrow)])
        rest_begins, rest_places, rest_size = (0,), nowhere, made
    rest = project(
        rest_places, rest_parts, rest_begins, rest_size, None, biases_rest, own[5], cosine, sine,
        slots, heads, [own_seen[3]],
    )
    if permuted:
        narrow_ref = lax.axis_index("narrow").astype(jnp.int32).reshape(1)
        mine = turn_pieces(narrow_ref, layer_pieces, [rest[1]])
        side, ahead, core_mine = flip(mine, 2), flip(mine, 4), flip(mine, 1)
        rest_seen = attend(rest, 0, heads, [], [mine])
        rest_seen = attend(rest, heads, heads, rest_seen, [])
        cut_row = (sum(sizes) // 2 + 7) // 8 * 8
        upper, lower = halve_pieces(side, ahead, cut_row, [rest_seen[3]])
        across = [flip(upper, 4), flip(lower, 2)]
        rest_seen = attend(rest, 2 * heads, (narrow - 3) * heads, rest_seen, [upper])
        joined = join_pieces(*across, [rest_seen[3]])
        layer_parts = [mine, side, ahead, joined]
        layer_parts += [core_mine] + [flip(value, 1) for value in (side, ahead, joined)]
        layer_begins = (0,) * 8
        layer_places = scattered((0, 2, 4, 6, 1, 3, 5, 7))
    else:
        rest_seen = attend(rest, 0, (narrow - 1) * heads, [], [])
        blocks = [up_weight, down_weight, out_weight]
        sizes = tuple(block.shape[0] for block in blocks)
        layer_parts = [
            jnp.concatenate([gathered(block, range(1, narrow)) for block in blocks], axis=1)
        ]
        layer_begins, layer_places = (0,), nowhere
    (
        layer_out,
        summed_grad,
        upweight_grad,
        downweight_grad,
        outweight_grad,
        small,
        own_grad,
        rest_grad,
    ) = layer(
        layer_places,
        ends,
        [own_seen[1], rest_seen[1]],
        tokens,
        cotangent,
        vectors,
        [biases_own, biases_rest],
        out_weight,
        up_weight,
        down_weight,
        layer_parts,
        layer_begins,
        sizes,
    )

    def back(made_arrays, seen, grad):
        return attend_back(
            seen[0], made_arrays[4], made_arrays[2], made_arrays[0], seen[2], grad, seen[3],
            cosine, sine, heads,
        )

    own_back, own_sums = back(own, own_seen, own_grad)
    own_all = own_grads(turn, own_back, tokens, outweight_grad, small, own_sums)
    upweight_grad, downweight_grad, query_grad, key_grad, value_grad, tail = lax.psum(
        (upweight_grad, downweight_grad, *own_all), "wide"
    )
    small = tail[width:]
    rest_back, _ = back(rest, rest_seen, rest_grad)
    tokens_grad = tokens_back(
        summed_grad,
        [value.reshape(-1, count) for value in (own_back, rest_back)],
        [packed_own, rest[5]],
    )
    return (
        layer_out,
        tokens_grad,
        query_grad.T,
        small[8, :width],
        key_grad.T,
        small[9, :width],
        value_grad.T,
        small[10, :width],
        tail[:width],
        small[6],
        small[4],
        small[5],
        upweight_grad,
        small[0],
        downweight_grad,
        small[1],
        small[2],
        small[3],
    )


def solution(mesh):
    in_specs = (
        P("wide", None),
        P("wide", None),
        P("wide", None),
        P(None, "narrow"),
        P("narrow"),
        P(None, "narrow"),
        P("narrow"),
        P(None, "narrow"),
        P("narrow"),
        P("narrow", None),
        P(),
        P(),
        P(),
        P(None, "narrow"),
        P("narrow"),
        P("narrow", None),
        P(),
        P(),
        P(),
    )
    out_specs = (
        P("wide", None),
        P("wide", None),
        P(None, "narrow"),
        P("narrow"),
        P(None, "narrow"),
        P("narrow"),
        P(None, "narrow"),
        P("narrow"),
        P("narrow", None),
        P(),
        P(),
        P(),
        P(None, "narrow"),
        P("narrow"),
        P("narrow", None),
        P(),
        P(),
        P(),
    )
    return jax.shard_map(body, mesh=mesh, in_specs=in_specs, out_specs=out_specs, check_vma=False)
```
